768 devices in a mesh: group: 24 (over z, core), member: 32 (over y, x).
Axes of the slice: x: 4, y: 8, z: 12, core: 2. Of those that a mesh axis runs over, the one named last changes fastest.
Arguments:
- features: bfloat16 [393216, 512], P(('group', 'member')), may hold values from -6 to 6
- w_self: bfloat16 [512, 512], replicated, may hold values from -0.25 to 0.25
- w_neigh: bfloat16 [512, 512], replicated, may hold values from -0.25 to 0.25
- bias: float32 [512], replicated, may hold values from -3 to 3
- set_members: int32 [196608, 8], P(('group', 'member')), may hold values from 0 to 511
- set_size: int32 [196608], P(('group', 'member')), may hold values from 1 to 8
- cross_list: int32 [24, 32, 24, 16], P('group', 'member'), may hold values from 0 to 255
- inner_list: int32 [24, 32, 32, 16], P('group', 'member'), may hold values from 0 to 383
- ref_slot: int32 [393216, 8], P(('group', 'member')), may hold values from 0 to 511
- ref_count: int32 [393216], P(('group', 'member')), may hold values from 1 to 8
- cotangent: bfloat16 [393216, 512], P(('group', 'member')), may hold values from -6 to 6
Outputs:
- output: bfloat16 [393216, 512], P(('group', 'member'))
- grad_features: bfloat16 [393216, 512], P(('group', 'member'))
- grad_w_self: float32 [512, 512], replicated
- grad_w_neigh: float32 [512, 512], replicated
- grad_bias: float32 [512], replicated
The draws below stay inside these ranges and needn't reach their ends.
All inputs are finite; a program needn't handle non-finite values.
Results may differ from the reference program's by a relative error of at most 0.0066.
Values may be sent and summed in bfloat16 or wider, within the bound.
A program may use at most 32 MiB of HBM per device.

```python
import jax
import jax.numpy as jnp
from jax import lax

D = 512
NODE_DEV = 512
SET_MOST = 8
REFS = 8
SET_DEV = 256
CAPG = 16
CAPM = 16
NODES = 393216
SETS = 196608
N_GROUP = 24
N_MEMBER = 32


def with_ends(values, stream_key, low, high):
    longest = values.shape.index(max(values.shape))
    spots = []
    for shift in (0, 1):
        where = [jax.random.randint(jax.random.fold_in(stream_key, axis), (), 0, length) for axis, length in enumerate(values.shape)]
        where[longest] = (where[longest] + shift) % values.shape[longest]
        spots.append(tuple(where))
    return values.at[spots[0]].set(low).at[spots[1]].set(high)


def level_of(key, extent, split, least, largest):
    gain, own = 1.0, jax.random.fold_in(key, 6)
    for dim, parts in split:
        heights = jnp.exp(jax.random.uniform(jax.random.fold_in(own, dim), (parts,), jnp.float32, least / len(split), largest / len(split)))
        gain = gain * jnp.repeat(heights, extent[dim] // parts).reshape([-1 if axis == dim else 1 for axis in range(len(extent))])
    return gain


def normal_values(own_key, extent, deviation, limit, split=(), kind=jnp.bfloat16):
    level = level_of(own_key, extent, split, -0.22, 0.18) if split else 1.0
    values = jax.random.normal(own_key, extent, jnp.float32) * deviation * level
    return jnp.minimum(jnp.maximum(values, -limit), limit).astype(kind)


def setup_inputs(seed: int = 0) -> dict:
    keys = jax.random.split(jax.random.key(seed), 12)
    return {
        "features": normal_values(keys[0], (NODES, D), 1.0, 6.0, ((0, 768),)),
        "w_self": normal_values(keys[1], (D, D), D ** -0.5, 0.25),
        "w_neigh": normal_values(keys[2], (D, D), D ** -0.5, 0.25),
        "bias": normal_values(keys[3], (D,), 0.5, 3.0, (), jnp.float32),
        "set_members": with_ends(jax.random.randint(keys[4], (SETS, SET_MOST), 0, NODE_DEV), jax.random.fold_in(keys[4], 1), 0, NODE_DEV - 1).astype(jnp.int32),
        "set_size": with_ends(jax.random.randint(keys[5], (SETS,), 1, SET_MOST + 1), jax.random.fold_in(keys[5], 1), 1, SET_MOST).astype(jnp.int32),
        "cross_list": with_ends(jax.random.randint(keys[6], (N_GROUP, N_MEMBER, N_GROUP, CAPG), 0, SET_DEV), jax.random.fold_in(keys[6], 1), 0, SET_DEV - 1).astype(jnp.int32),
        "inner_list": with_ends(jax.random.randint(keys[7], (N_GROUP, N_MEMBER, N_MEMBER, CAPM), 0, N_GROUP * CAPG), jax.random.fold_in(keys[7], 1), 0, (N_GROUP * CAPG) - 1).astype(jnp.int32),
        "ref_slot": with_ends(jax.random.randint(keys[8], (NODES, REFS), 0, N_MEMBER * CAPM), jax.random.fold_in(keys[8], 1), 0, (N_MEMBER * CAPM) - 1).astype(jnp.int32),
        "ref_count": with_ends(jax.random.randint(keys[9], (NODES,), 1, REFS + 1), jax.random.fold_in(keys[9], 1), 1, REFS).astype(jnp.int32),
        "cotangent": normal_values(keys[10], (NODES, D), 1.0, 6.0, ((0, 768),)),
    }


def reference(features, w_self, w_neigh, bias, set_members, set_size, cross_list, inner_list, ref_slot, ref_count, cotangent):
    device_total = N_GROUP * N_MEMBER
    feats = features.reshape(device_total, NODE_DEV, D)
    member_ids = set_members.reshape(device_total, SET_DEV, SET_MOST)
    sizes = set_size.reshape(device_total, SET_DEV)
    slots = ref_slot.reshape(device_total, NODE_DEV, REFS)
    counts = ref_count.reshape(device_total, NODE_DEV)
    cotan = cotangent.reshape(device_total, NODE_DEV, D)
    devices = jnp.arange(device_total, dtype=jnp.int32)

    def aggregate(item):
        local_feats, local_members, local_sizes = item
        total = jnp.zeros((SET_DEV, D), jnp.float32)
        for position in range(SET_MOST):
            rows = local_feats[local_members[:, position]].astype(jnp.float32)
            total = total + jnp.where((position < local_sizes)[:, None], rows, 0.0)
        return total.astype(jnp.bfloat16)

    agg = lax.map(aggregate, (feats, member_ids, sizes))
    agg_flat = agg.reshape(device_total * SET_DEV, D)

    def forward(carry, item):
        device, local_feats, local_slots, local_counts, local_cotan = item
        group_at = device // N_MEMBER
        member_at = device % N_MEMBER
        rows = inner_list[group_at, :, member_at, :]
        src_group = rows // CAPG
        src_col = rows % CAPG
        passer = jnp.arange(N_MEMBER, dtype=jnp.int32)[:, None]
        chosen = cross_list[src_group, passer, group_at, src_col]
        flat = ((src_group * N_MEMBER + passer) * SET_DEV + chosen).reshape(-1)
        arrived = agg_flat[flat]
        count_f = local_counts.astype(jnp.float32)
        total = jnp.zeros((NODE_DEV, D), jnp.float32)
        for which in range(REFS):
            live = (which < local_counts)[:, None]
            total = total + jnp.where(live, arrived[local_slots[:, which]].astype(jnp.float32), 0.0)
        neigh = (total / count_f[:, None]).astype(jnp.bfloat16)
        preact = jnp.dot(local_feats, w_self, preferred_element_type=jnp.float32) + jnp.dot(neigh, w_neigh, preferred_element_type=jnp.float32) + bias.astype(jnp.float32)
        gate_val = jax.nn.sigmoid(preact)
        output = (preact * gate_val).astype(jnp.bfloat16)
        grad_full = local_cotan.astype(jnp.float32) * gate_val * (1.0 + preact * (1.0 - gate_val))
        grad_low = grad_full.astype(jnp.bfloat16)
        grad_ws = jnp.dot(local_feats.T, grad_low, preferred_element_type=jnp.float32)
        grad_wn = jnp.dot(neigh.T, grad_low, preferred_element_type=jnp.float32)
        grad_b = jnp.sum(grad_full, axis=0)
        grad_neigh = jnp.dot(grad_low, w_neigh.T, preferred_element_type=jnp.float32) / count_f[:, None]
        grad_slot = jnp.zeros((N_MEMBER * CAPM, D), jnp.float32)
        for which in range(REFS):
            live = (which < local_counts)[:, None]
            grad_slot = grad_slot.at[local_slots[:, which]].add(jnp.where(live, grad_neigh, 0.0))
        new_carry = (carry[0] + grad_ws, carry[1] + grad_wn, carry[2] + grad_b)
        return new_carry, (output, grad_slot.astype(jnp.bfloat16), grad_low)

    start = (jnp.zeros((D, D), jnp.float32), jnp.zeros((D, D), jnp.float32), jnp.zeros((D,), jnp.float32))
    sums, outs = lax.scan(forward, start, (devices, feats, slots, counts, cotan))
    output, grad_slots, grad_lows = outs
    slot_grid = grad_slots.reshape(N_GROUP, N_MEMBER, N_MEMBER, CAPM, D)
    inner_flat = inner_list.reshape(device_total, N_MEMBER * CAPM)

    def relay_back(device):
        group_at = device // N_MEMBER
        member_at = device % N_MEMBER
        part = slot_grid[group_at, :, member_at].reshape(N_MEMBER * CAPM, D).astype(jnp.float32)
        return jnp.zeros((N_GROUP * CAPG, D), jnp.float32).at[inner_flat[device]].add(part).astype(jnp.bfloat16)

    grad_relay = lax.map(relay_back, devices)
    relay_grid = grad_relay.reshape(N_GROUP, N_MEMBER, N_GROUP, CAPG, D)
    cross_flat = cross_list.reshape(device_total, N_GROUP * CAPG)

    def source_back(device):
        group_at = device // N_MEMBER
        member_at = device % N_MEMBER
        part = relay_grid[:, member_at, group_at].reshape(N_GROUP * CAPG, D).astype(jnp.float32)
        return jnp.zeros((SET_DEV, D), jnp.float32).at[cross_flat[device]].add(part).astype(jnp.bfloat16)

    grad_agg = lax.map(source_back, devices)

    def feature_back(item):
        grad_low, local_members, local_sizes, local_agg = item
        result = jnp.dot(grad_low, w_self.T, preferred_element_type=jnp.float32)
        spread = local_agg.astype(jnp.float32)
        for position in range(SET_MOST):
            live = (position < local_sizes)[:, None]
            result = result.at[local_members[:, position]].add(jnp.where(live, spread, 0.0))
        return result.astype(jnp.bfloat16)

    grad_features = lax.map(feature_back, (grad_lows, member_ids, sizes, grad_agg))
    return (output.reshape(NODES, D), grad_features.reshape(NODES, D), sums[0], sums[1], sums[2])
```

```python
import functools

import jax
import jax.numpy as jnp
from jax import lax
from jax.experimental import pallas as pl
from jax.experimental.pallas import tpu as pltpu
from jax.sharding import PartitionSpec as P

MESH = pl.DeviceIdType.MESH
BF = jnp.bfloat16
F32 = jnp.float32
CORES = 2


def dot(a, b, ca=1, cb=0):
    return lax.dot_general(a, b, (((ca,), (cb,)), ((), ())), preferred_element_type=F32)


def kernel(
    groups, members, nx, cap,
    feats, w_self, w_neigh, bias, mem_live, ref_live, cross_row, inner_row, cot,
    out, gfeat, gws, gwn, gbias,
    member_of, ref_of, cross_t, inner_t, send_z, relay, send_m, arrived,
    neigh, low, pre, own, split, back_m, returned, back_z, homeward,
    part, core_send, core_recv, x_send, x_recv, y_send, y_recv, z_recv, whole,
    bias_own, bias_core, bias_x, bias_y, bias_z,
    ssem, rsem,
):
    g = lax.axis_index("group")
    m = lax.axis_index("member")
    z, core = g // CORES, g % CORES
    y, x = m // nx, m % nx
    nz, ny = groups // CORES, members // nx
    nodes, width = feats.shape
    sets = mem_live.shape[0]

    barrier = pltpu.get_barrier_semaphore()

    def greet(axis, count, me):
        def body(k, c):
            peer = lax.rem(me + k, count)
            pl.semaphore_signal(barrier, inc=1, device_id={axis: peer}, device_id_type=MESH)
            return c
        lax.fori_loop(1, count, body, 0)

    greet("group", groups, g)
    greet("member", members, m)

    def remote(src, dst, which, target):
        return pltpu.make_async_remote_copy(
            src_ref=src, dst_ref=dst, send_sem=ssem.at[which], recv_sem=rsem.at[which],
            device_id=target, device_id_type=MESH,
        )

    def landed(ref, which):
        pltpu.make_async_copy(ref, ref, rsem.at[which]).wait()

    def left(ref, which):
        pltpu.make_async_copy(ref, ref, ssem.at[which]).wait()

    def exchange(src, dst, which, axis, count, me):
        def body(k, c):
            peer = lax.rem(me + k, count)
            at = pl.multiple_of(peer * cap, cap)
            to = pl.multiple_of(me * cap, cap)
            remote(src.at[pl.ds(at, cap)], dst.at[pl.ds(to, cap)], which, {axis: peer}).start()
            return c
        lax.fori_loop(1, count, body, 0)
        mine = pl.ds(pl.multiple_of(me * cap, cap), cap)
        dst[mine, :] = src[mine, :]

    lane = lax.broadcasted_iota(jnp.int32, (sets, nodes), 1)
    acc = jnp.zeros((sets, nodes), F32)
    for k in range(mem_live.shape[1]):
        acc += jnp.where(mem_live[:, k:k + 1] == lane, 1.0, 0.0)
    member_of[...] = acc.astype(BF)
    agg = dot(member_of[...], feats[...]).astype(BF)
    relays = groups * cap
    sub = lax.broadcasted_iota(jnp.int32, (sets, relays), 0)
    cross_t[...] = jnp.where(cross_row[...] == sub, 1.0, 0.0).astype(BF)
    send_z[...] = dot(cross_t[...], agg, 0, 0).astype(BF)

    pl.semaphore_wait(barrier, groups + members - 2)
    exchange(send_z, relay, 0, "group", groups, g)

    slots = members * cap
    sub = lax.broadcasted_iota(jnp.int32, (relays, slots), 0)
    inner_t[...] = jnp.where(inner_row[...] == sub, 1.0, 0.0).astype(BF)
    blk = 128
    for b in range(nodes // blk):
        rows = slice(b * blk, (b + 1) * blk)
        lane = lax.broadcasted_iota(jnp.int32, (blk, slots), 1)
        acc = jnp.zeros((blk, slots), F32)
        for k in range(ref_live.shape[1]):
            acc += jnp.where(ref_live[rows, k:k + 1] == lane, 1.0, 0.0)
        ref_of[rows, :] = acc.astype(BF)
    pre[...] = dot(feats[...], w_self[...]) + bias[...]

    landed(relay.at[pl.ds(0, (groups - 1) * cap)], 0)
    send_m[...] = dot(inner_t[...], relay[...], 0, 0).astype(BF)
    exchange(send_m, arrived, 1, "member", members, m)
    landed(arrived.at[pl.ds(0, (members - 1) * cap)], 1)

    total_b = jnp.zeros((1, width), F32)
    for b in range(nodes // blk):
        rows = slice(b * blk, (b + 1) * blk)
        count = jnp.sum(jnp.where(ref_live[rows, :] >= 0, 1.0, 0.0), axis=1, keepdims=True)
        mean = (dot(ref_of[rows, :], arrived[...]) / count).astype(BF)
        neigh[rows, :] = mean
        p = pre[rows, :] + dot(mean, w_neigh[...])
        gate = jax.nn.sigmoid(p)
        out[rows, :] = (p * gate).astype(BF)
        full = cot[rows, :].astype(F32) * gate * (1.0 + p * (1.0 - gate))
        total_b = total_b + jnp.sum(full, axis=0, keepdims=True)
        lowb = full.astype(BF)
        low[rows, :] = lowb
        gn = dot(lowb, w_neigh[...], 1, 1) / count
        hi = gn.astype(BF)
        split[0, rows, :] = hi
        split[1, rows, :] = (gn - hi.astype(F32)).astype(BF)
    back_m[...] = (dot(ref_of[...], split[0], 0, 0) + dot(ref_of[...], split[1], 0, 0)).astype(BF)
    exchange(back_m, returned, 2, "member", members, m)

    part[0] = dot(feats[...], low[...], 0, 0)
    part[1] = dot(neigh[...], low[...], 0, 0)
    sibling = {"group": z * CORES + 1 - core}
    core_send[...] = part[1 - core].astype(BF)
    bias_own[...] = jnp.zeros_like(bias_own)
    for i in range(width // 128):
        bias_own[i:i + 1, :] = total_b[:, i * 128:(i + 1) * 128]
    core_copy = remote(core_send, core_recv, 3, sibling)
    core_copy.start()
    bias_copy = remote(bias_own, bias_core, 4, sibling)
    bias_copy.start()
    own[...] = dot(low[...], w_self[...], 1, 1)
    core_copy.wait()
    bias_copy.wait()

    chunk = width // nx

    def peers(count, me, go):
        def body(k, c):
            go(lax.rem(me + k, count))
            return c
        lax.fori_loop(1, count, body, 0)

    def x_target(p):
        return {"member": y * nx + p}

    def y_target(p):
        return {"member": p * nx + x}

    def z_target(p):
        return {"group": p * CORES + core}

    x_send[...] = (part[core] + core_recv[...].astype(F32)).astype(BF)
    bias_x[x] = bias_own[...] + bias_core[...]

    def go(p):
        at = pl.multiple_of(p * chunk, chunk)
        remote(x_send.at[pl.ds(at, chunk)], x_recv.at[x], 5, x_target(p)).start()
        remote(bias_x.at[x], bias_x.at[x], 6, x_target(p)).start()
    peers(nx, x, go)

    landed(returned.at[pl.ds(0, (members - 1) * cap)], 2)
    back_z[...] = dot(inner_t[...], returned[...]).astype(BF)
    exchange(back_z, homeward, 7, "group", groups, g)

    x_rows = pl.ds(pl.multiple_of(x * chunk, chunk), chunk)
    landed(x_recv.at[pl.ds(0, nx - 1)], 5)
    landed(bias_x.at[pl.ds(0, nx - 1)], 6)
    x_recv[x] = x_send[x_rows, :]
    acc = x_recv[0].astype(F32)
    for i in range(1, nx):
        acc += x_recv[i].astype(F32)
    y_send[...] = acc.astype(BF)
    acc = bias_x[0]
    for i in range(1, nx):
        acc += bias_x[i]
    bias_y[y] = acc

    piece = chunk // ny

    def go(p):
        at = pl.multiple_of(p * piece, piece)
        remote(y_send.at[pl.ds(at, piece)], y_recv.at[y], 8, y_target(p)).start()
        remote(bias_y.at[y], bias_y.at[y], 9, y_target(p)).start()
    peers(ny, y, go)
    landed(y_recv.at[pl.ds(0, ny - 1)], 8)
    landed(bias_y.at[pl.ds(0, ny - 1)], 9)
    y_rows = pl.ds(pl.multiple_of(y * piece, piece), piece)
    y_recv[y] = y_send[y_rows, :]
    acc = y_recv[0].astype(F32)
    for i in range(1, ny):
        acc += y_recv[i].astype(F32)
    z_recv[z] = acc.astype(BF)
    acc = bias_y[0]
    for i in range(1, ny):
        acc += bias_y[i]
    bias_z[z] = acc

    def go(p):
        remote(z_recv.at[z], z_recv.at[z], 10, z_target(p)).start()
        remote(bias_z.at[z], bias_z.at[z], 11, z_target(p)).start()
    peers(nz, z, go)
    landed(z_recv.at[pl.ds(0, nz - 1)], 10)
    landed(bias_z.at[pl.ds(0, nz - 1)], 11)
    acc = z_recv[0].astype(F32)
    for i in range(1, nz):
        acc += z_recv[i].astype(F32)
    piece_rows = pl.ds(pl.multiple_of(x * chunk + y * piece, piece), piece)
    whole[core, piece_rows, :] = acc.astype(BF)
    acc = bias_z[0]
    for i in range(1, nz):
        acc += bias_z[i]
    for i in range(width // 128):
        gbias[:, i * 128:(i + 1) * 128] = acc[i:i + 1, :]

    def go(p):
        ref = whole.at[core, piece_rows]
        remote(ref, ref, 12, y_target(p)).start()
    peers(ny, y, go)

    landed(homeward.at[pl.ds(0, (groups - 1) * cap)], 7)
    grad_agg = dot(cross_t[...], homeward[...]).astype(BF)
    gfeat[...] = (own[...] + dot(member_of[...], grad_agg, 0, 0)).astype(BF)

    landed(whole.at[0, pl.ds(0, (ny - 1) * piece)], 12)

    def go(p):
        ref = whole.at[core, x_rows]
        remote(ref, ref, 13, x_target(p)).start()
    peers(nx, x, go)
    landed(whole.at[0, pl.ds(0, (nx - 1) * chunk)], 13)
    last = remote(whole.at[core], whole.at[core], 14, sibling)
    last.start()
    landed(whole.at[0], 14)
    gws[...] = whole[0].astype(F32)
    gwn[...] = whole[1].astype(F32)

    left(send_z.at[pl.ds(0, (groups - 1) * cap)], 0)
    left(send_m.at[pl.ds(0, (members - 1) * cap)], 1)
    left(back_m.at[pl.ds(0, (members - 1) * cap)], 2)
    left(x_recv.at[pl.ds(0, nx - 1)], 5)
    left(bias_x.at[pl.ds(0, nx - 1)], 6)
    left(back_z.at[pl.ds(0, (groups - 1) * cap)], 7)
    left(y_recv.at[pl.ds(0, ny - 1)], 8)
    left(bias_y.at[pl.ds(0, ny - 1)], 9)
    left(z_recv.at[pl.ds(0, nz - 1)], 10)
    left(bias_z.at[pl.ds(0, nz - 1)], 11)
    left(whole.at[0, pl.ds(0, (ny - 1) * piece)], 12)
    left(whole.at[0, pl.ds(0, (nx - 1) * chunk)], 13)
    left(whole.at[0], 14)


def shards(
    nx, features, w_self, w_neigh, bias, set_members, set_size, cross_list, inner_list,
    ref_slot, ref_count, cotangent,
):
    nodes, width = features.shape
    sets, most = set_members.shape
    groups = lax.axis_size("group")
    members = lax.axis_size("member")
    refs = ref_slot.shape[1]
    cap = cross_list.shape[3]
    ny, nz = members // nx, groups // CORES
    mem_live = jnp.where(jnp.arange(most, dtype=jnp.int32)[None, :] < set_size[:, None], set_members, -1)
    ref_live = jnp.where(jnp.arange(refs, dtype=jnp.int32)[None, :] < ref_count[:, None], ref_slot, -1)
    cross_row = cross_list.reshape(1, groups * cap)
    inner_row = inner_list.reshape(1, members * cap)
    chunk = width // nx
    piece = chunk // ny
    vmem = pl.BlockSpec(memory_space=pltpu.VMEM)
    S = jax.ShapeDtypeStruct
    outs = pl.pallas_call(
        functools.partial(kernel, groups, members, nx, cap),
        out_shape=(
            S((nodes, width), BF), S((nodes, width), BF), S((width, width), F32),
            S((width, width), F32), S((1, width), F32),
        ),
        in_specs=[vmem] * 9,
        out_specs=(vmem,) * 5,
        scratch_shapes=[
            pltpu.VMEM((sets, nodes), BF),
            pltpu.VMEM((nodes, members * cap), BF),
            pltpu.VMEM((sets, groups * cap), BF),
            pltpu.VMEM((groups * cap, members * cap), BF),
            pltpu.VMEM((groups * cap, width), BF),
            pltpu.VMEM((groups * cap, width), BF),
            pltpu.VMEM((members * cap, width), BF),
            pltpu.VMEM((members * cap, width), BF),
            pltpu.VMEM((nodes, width), BF),
            pltpu.VMEM((nodes, width), BF),
            pltpu.VMEM((nodes, width), F32),
            pltpu.VMEM((nodes, width), F32),
            pltpu.VMEM((2, nodes, width), BF),
            pltpu.VMEM((members * cap, width), BF),
            pltpu.VMEM((members * cap, width), BF),
            pltpu.VMEM((groups * cap, width), BF),
            pltpu.VMEM((groups * cap, width), BF),
            pltpu.VMEM((2, width, width), F32),
            pltpu.VMEM((width, width), BF),
            pltpu.VMEM((width, width), BF),
            pltpu.VMEM((width, width), BF),
            pltpu.VMEM((nx, chunk, width), BF),
            pltpu.VMEM((chunk, width), BF),
            pltpu.VMEM((ny, piece, width), BF),
            pltpu.VMEM((nz, piece, width), BF),
            pltpu.VMEM((2, width, width), BF),
            pltpu.VMEM((8, 128), F32),
            pltpu.VMEM((8, 128), F32),
            pltpu.VMEM((nx, 8, 128), F32),
            pltpu.VMEM((ny, 8, 128), F32),
            pltpu.VMEM((nz, 8, 128), F32),
            pltpu.SemaphoreType.DMA((15,)),
            pltpu.SemaphoreType.DMA((15,)),
        ],
        compiler_params=pltpu.CompilerParams(
            collective_id=0, has_side_effects=True, vmem_limit_bytes=48 * 2**20
        ),
    )(features, w_self, w_neigh, bias.reshape(1, width), mem_live, ref_live, cross_row, inner_row, cotangent)
    output, gfeat, gws, gwn, gbias = outs
    return output, gfeat, gws, gwn, gbias.reshape(width)


def solution(mesh):
    nx = 4
    in_specs = (
        P(("group", "member"), None),
        P(),
        P(),
        P(),
        P(("group", "member"), None),
        P(("group", "member")),
        P("group", "member", None, None),
        P("group", "member", None, None),
        P(("group", "member"), None),
        P(("group", "member")),
        P(("group", "member"), None),
    )
    out_specs = (P(("group", "member"), None), P(("group", "member"), None), P(), P(), P())
    return jax.shard_map(
        functools.partial(shards, nx), mesh=mesh, in_specs=in_specs, out_specs=out_specs, check_vma=False
    )
```

```python
import functools

import jax
import jax.numpy as jnp
from jax import lax
from jax.experimental import pallas as pl
from jax.experimental.pallas import tpu as pltpu
from jax.sharding import PartitionSpec as P

MESH = pl.DeviceIdType.MESH
BF = jnp.bfloat16
F32 = jnp.float32
I32 = jnp.int32
CORES = 2
NCH = 2


def dot(a, b, ca=1, cb=0):
    return lax.dot_general(a, b, (((ca,), (cb,)), ((), ())), preferred_element_type=F32)


def iota(shape, dim):
    return lax.broadcasted_iota(I32, shape, dim)


def flat_row(table):
    cap, n = table.shape
    expand = jnp.where(iota((n, n * cap), 1) // cap == iota((n, n * cap), 0), 1.0, 0.0).astype(BF)
    high = dot((table // 16).astype(F32).astype(BF), expand)
    low = dot((table % 16).astype(F32).astype(BF), expand)
    keep = iota((cap, n * cap), 1) % cap == iota((cap, n * cap), 0)
    return jnp.sum(jnp.where(keep, high * 16.0 + low, 0.0), axis=0, keepdims=True).astype(I32)


def hits(table, count, first, rows):
    entries, n = table.shape
    live = jnp.where(iota((entries, n), 0) < count, table, -1)
    sub = iota((rows, n), 0) + first
    acc = jnp.zeros((rows, n), F32)
    for k in range(entries):
        acc += jnp.where(live[k:k + 1, :] == sub, 1.0, 0.0)
    return acc.astype(BF)


def z_near(nz):
    return 4 if nz % 4 == 0 else nz


def kernel(
    groups, members, nx, cap,
    feats_h, w_self_h, w_neigh_h, bias_h, mem_h, size_h, cross_h, inner_h, ref_h, count_h, cot_h,
    out_h, gfeat_h, grads_h, gbias_h,
    feats, w_self, w_neigh, bias, mem, size, cross, inner, ref, count, cot,
    member_t, member_n, ref_t, ref_n, cross_t, cross_n, inner_t, inner_n, feats_t, inv,
    send_z, relay, send_m, arrived,
    neigh, low, pre, own, split, back_m, returned, back_z, homeward,
    neigh_t, part, core_send, core_recv, x_send, x_recv, y_full, y_send, y_recv, z_recv, z_last, whole,
    out, gfeat, gbias,
    bias_own, bias_core, bias_x, bias_y, bias_z, bias_zl,
    lsem, osem, ssem, rsem, fsem, gsem,
):
    g = lax.axis_index("group")
    m = lax.axis_index("member")
    z, core = g // CORES, g % CORES
    y, x = m // nx, m % nx
    nz, ny = groups // CORES, members // nx
    near = z_near(nz)
    runs = nz // near
    nodes, width = feats.shape
    sets = mem.shape[1]
    wide = width // NCH
    relays, slots = groups * cap, members * cap
    pairs = (
        (mem_h, mem), (size_h, size), (cross_h, cross), (feats_h, feats), (inner_h, inner), (ref_h, ref),
        (count_h, count), (w_self_h, w_self), (bias_h, bias), (w_neigh_h, w_neigh), (cot_h, cot),
    )
    loads = [pltpu.make_async_copy(a, b, lsem.at[i]) for i, (a, b) in enumerate(pairs)]
    for load in loads:
        load.start()

    barrier = pltpu.get_barrier_semaphore()

    def around(count, me, go):
        def body(k, c):
            s = (k + 1) // 2
            go(lax.rem(jnp.where(k % 2 == 1, me + s, me - s + count), count))
            return c
        lax.fori_loop(1, count, body, 0)

    def greet(axis, count, me):
        def go(peer):
            pl.semaphore_signal(barrier, inc=1, device_id={axis: peer}, device_id_type=MESH)
        around(count, me, go)

    greet("group", groups, g)
    greet("member", members, m)

    def remote(src, dst, sems, which, target):
        return pltpu.make_async_remote_copy(
            src_ref=src, dst_ref=dst, send_sem=sems[0].at[which], recv_sem=sems[1].at[which],
            device_id=target, device_id_type=MESH,
        )

    def done(ref, sem):
        pltpu.make_async_copy(ref, ref, sem).wait()

    rows_sems = (fsem, gsem)

    def exchange(src, dst, which, axis, count, me):
        def go(peer):
            at = pl.multiple_of(peer * cap, cap)
            to = pl.multiple_of(me * cap, cap)
            remote(src.at[pl.ds(at, cap)], dst.at[pl.ds(to, cap)], rows_sems, which, {axis: peer}).start()
        around(count, me, go)
        mine = pl.ds(pl.multiple_of(me * cap, cap), cap)
        dst[mine, :] = src[mine, :]

    def others(buf, count):
        return buf.at[0, pl.ds(0, (count - 1) * cap)]

    blk = 64
    loads[0].wait()
    loads[1].wait()
    for b in range(nodes // blk):
        member_t[b * blk:(b + 1) * blk, :] = hits(mem[...], size[...], b * blk, blk)
    member_n[...] = member_t[...].T
    loads[2].wait()
    cross_t[...] = jnp.where(flat_row(cross[...]) == iota((sets, relays), 0), 1.0, 0.0).astype(BF)
    cross_n[...] = cross_t[...].T
    loads[3].wait()
    for h in range(NCH):
        cols = slice(h * wide, (h + 1) * wide)
        agg = dot(member_n[...], feats[:, cols]).astype(BF)
        send_z[h] = dot(cross_n[...], agg).astype(BF)
        if h == 0:
            pl.semaphore_wait(barrier, groups + members - 2)
        exchange(send_z.at[h], relay.at[h], h, "group", groups, g)

    loads[4].wait()
    inner_t[...] = jnp.where(flat_row(inner[...]) == iota((relays, slots), 0), 1.0, 0.0).astype(BF)
    inner_n[...] = inner_t[...].T
    loads[5].wait()
    loads[6].wait()
    blk = 32
    for b in range(slots // blk):
        ref_t[b * blk:(b + 1) * blk, :] = hits(ref[...], count[...], b * blk, blk)
    ref_n[...] = ref_t[...].T
    inv[...] = jnp.broadcast_to(1.0 / count[...].astype(F32), (128, nodes)).T
    feats_t[...] = feats[...].T
    loads[7].wait()
    loads[8].wait()
    pre[...] = dot(feats[...], w_self[...]) + bias[...]
    loads[9].wait()
    loads[10].wait()

    for h in range(NCH):
        done(others(relay, groups), gsem.at[h])
        send_m[h] = dot(inner_n[...], relay[h]).astype(BF)
        exchange(send_m.at[h], arrived.at[h], NCH + h, "member", members, m)

    blk = 128
    total_b = jnp.zeros((1, width), F32)
    for h in range(NCH):
        done(others(arrived, members), gsem.at[NCH + h])
        cols = slice(h * wide, (h + 1) * wide)
        for b in range(nodes // blk):
            rows = slice(b * blk, (b + 1) * blk)
            mean = (dot(ref_n[rows, :], arrived[h]) * inv[rows, 0:1]).astype(BF)
            neigh[rows, cols] = mean
            p = pre[rows, :] + dot(mean, w_neigh[cols, :])
            if h < NCH - 1:
                pre[rows, :] = p
                continue
            gate = jax.nn.sigmoid(p)
            out[rows, :] = (p * gate).astype(BF)
            full = cot[rows, :].astype(F32) * gate * (1.0 + p * (1.0 - gate))
            total_b = total_b + jnp.sum(full, axis=0, keepdims=True)
            low[rows, :] = full.astype(BF)

    sums = (ssem, rsem)
    chunk = width // nx
    piece = chunk // ny
    sibling = {"group": z * CORES + 1 - core}
    x_rows = pl.ds(pl.multiple_of(x * chunk, chunk), chunk)
    y_rows = pl.ds(pl.multiple_of(y * piece, piece), piece)
    piece_rows = pl.ds(pl.multiple_of(x * chunk + y * piece, piece), piece)
    spot, run = z % near, z // near
    bias_sem = 8 * NCH

    def ring(me, count, k):
        return lax.rem(me + k, count)

    def x_target(p):
        return {"member": y * nx + p}

    def y_target(p):
        return {"member": p * nx + x}

    def z_target(p):
        return {"group": p * CORES + core}

    def add_up(buf, n, first=None):
        acc = buf[0].astype(F32) if first is None else first + buf[0].astype(F32)
        for i in range(1, n):
            acc += buf[i].astype(F32)
        return acc

    def core_copy(h):
        return remote(core_send.at[h], core_recv.at[h], sums, h, sibling)

    def bias_copy():
        return remote(bias_own, bias_core, sums, bias_sem, sibling)

    def core_stage(h):
        cols = slice(h * wide, (h + 1) * wide)
        part[0, h] = dot(feats_t[...], low[:, cols])
        part[1, h] = dot(neigh_t[...], low[:, cols])
        core_send[h] = part[1 - core, h].astype(BF)
        core_copy(h).start()
        if h == 0:
            bias_own[...] = jnp.zeros_like(bias_own)
            for i in range(width // 128):
                bias_own[i:i + 1, :] = total_b[:, i * 128:(i + 1) * 128]
            bias_copy().start()

    def x_stage(h):
        core_copy(h).wait()
        total = part[core, h] + core_recv[h].astype(F32)
        part[core, h] = total
        x_send[h] = total.astype(BF)
        for k in range(1, nx):
            p = ring(x, nx, k)
            at = pl.ds(pl.multiple_of(p * chunk, chunk), chunk)
            remote(x_send.at[h, at], x_recv.at[h, k - 1], sums, NCH + h, x_target(p)).start()
        if h == 0:
            bias_copy().wait()
            bias_x[x] = bias_own[...] + bias_core[...]
            for k in range(1, nx):
                p = ring(x, nx, k)
                remote(bias_x.at[x], bias_x.at[x], sums, bias_sem + 1, x_target(p)).start()

    def y_stage(h):
        done(x_recv.at[h], rsem.at[NCH + h])
        total = add_up(x_recv.at[h], nx - 1, part[core, h, x_rows, :])
        y_full[h] = total
        y_send[h] = total.astype(BF)
        for k in range(1, ny):
            p = ring(y, ny, k)
            at = pl.ds(pl.multiple_of(p * piece, piece), piece)
            remote(y_send.at[h, at], y_recv.at[h, k - 1], sums, 2 * NCH + h, y_target(p)).start()
        if h == 0:
            done(bias_x.at[pl.ds(0, nx - 1)], rsem.at[bias_sem + 1])
            bias_y[y] = add_up(bias_x, nx)
            for k in range(1, ny):
                p = ring(y, ny, k)
                remote(bias_y.at[y], bias_y.at[y], sums, bias_sem + 2, y_target(p)).start()

    def z_stage(h):
        done(y_recv.at[h], rsem.at[2 * NCH + h])
        z_recv[h, spot] = add_up(y_recv.at[h], ny - 1, y_full[h, y_rows, :]).astype(BF)
        for k in range(1, near):
            p = run * near + ring(spot, near, k)
            remote(z_recv.at[h, spot], z_recv.at[h, spot], sums, 3 * NCH + h, z_target(p)).start()
        if h == 0:
            done(bias_y.at[pl.ds(0, ny - 1)], rsem.at[bias_sem + 2])
            bias_z[spot] = add_up(bias_y, ny)
            for k in range(1, near):
                p = run * near + ring(spot, near, k)
                remote(bias_z.at[spot], bias_z.at[spot], sums, bias_sem + 3, z_target(p)).start()

    def z_next(h):
        done(z_recv.at[h, pl.ds(0, near - 1)], rsem.at[3 * NCH + h])
        z_last[h, run] = add_up(z_recv.at[h], near).astype(BF)
        for k in range(1, runs):
            p = ring(run, runs, k) * near + spot
            remote(z_last.at[h, run], z_last.at[h, run], sums, 4 * NCH + h, z_target(p)).start()
        if h == 0:
            done(bias_z.at[pl.ds(0, near - 1)], rsem.at[bias_sem + 3])
            bias_zl[run] = add_up(bias_z, near)
            for k in range(1, runs):
                p = ring(run, runs, k) * near + spot
                remote(bias_zl.at[run], bias_zl.at[run], sums, bias_sem + 4, z_target(p)).start()

    def y_back(h):
        done(z_last.at[h, pl.ds(0, runs - 1)], rsem.at[4 * NCH + h])
        whole[core, h, piece_rows, :] = add_up(z_last.at[h], runs).astype(BF)
        at = whole.at[core, h, piece_rows]
        for k in range(1, ny):
            remote(at, at, sums, 5 * NCH + h, y_target(ring(y, ny, k))).start()

    def x_back(h):
        done(whole.at[0, 0, pl.ds(0, (ny - 1) * piece)], rsem.at[5 * NCH + h])
        at = whole.at[core, h, x_rows]
        for k in range(1, nx):
            remote(at, at, sums, 6 * NCH + h, x_target(ring(x, nx, k))).start()

    def core_back(h):
        done(whole.at[0, 0, pl.ds(0, (nx - 1) * chunk)], rsem.at[6 * NCH + h])
        remote(whole.at[core, h], whole.at[core, h], sums, 7 * NCH + h, sibling).start()

    def member_back(h):
        cols = slice(h * wide, (h + 1) * wide)
        for b in range(nodes // blk):
            rows = slice(b * blk, (b + 1) * blk)
            gn = dot(low[rows, :], w_neigh[cols, :], 1, 1) * inv[rows, 0:1]
            hi = gn.astype(BF)
            split[0, rows, :] = hi
            split[1, rows, :] = (gn - hi.astype(F32)).astype(BF)
        back_m[h] = (dot(ref_t[...], split[0]) + dot(ref_t[...], split[1])).astype(BF)

    def member_send(h):
        exchange(back_m.at[h], returned.at[h], 2 * NCH + h, "member", members, m)

    def home(h):
        done(others(returned, members), gsem.at[2 * NCH + h])
        back_z[h] = dot(inner_t[...], returned[h]).astype(BF)
        exchange(back_z.at[h], homeward.at[h], 3 * NCH + h, "group", groups, g)

    def features_back(h):
        cols = slice(h * wide, (h + 1) * wide)
        done(others(homeward, groups), gsem.at[3 * NCH + h])
        grad_agg = dot(cross_t[...], homeward[h]).astype(BF)
        gfeat[:, cols] = (own[:, cols] + dot(member_t[...], grad_agg)).astype(BF)

    stores = [
        pltpu.make_async_copy(out, out_h, osem.at[0]),
        pltpu.make_async_copy(gfeat, gfeat_h, osem.at[1]),
        pltpu.make_async_copy(gbias, gbias_h, osem.at[2]),
        pltpu.make_async_copy(whole.at[core], grads_h.at[core], osem.at[3]),
    ]
    stores[0].start()
    neigh_t[...] = neigh[...].T
    for h in range(NCH):
        core_stage(h)
    for h in range(NCH):
        member_back(h)
        x_stage(h)
    member_send(0)
    own[...] = dot(low[...], w_self[...], 1, 1)
    for h in range(NCH):
        y_stage(h)
    member_send(1)
    home(0)
    for h in range(NCH):
        z_stage(h)
    for h in range(NCH):
        z_next(h)
    home(1)
    for h in range(NCH):
        y_back(h)
    for h in range(NCH):
        x_back(h)
    features_back(0)
    core_back(0)
    features_back(1)
    core_back(1)
    done(bias_zl.at[pl.ds(0, runs - 1)], rsem.at[bias_sem + 4])
    bias_sum = add_up(bias_zl, runs)
    for i in range(width // 128):
        gbias[:, i * 128:(i + 1) * 128] = bias_sum[i:i + 1, :]
    for store in stores[1:]:
        store.start()
    for h in range(NCH):
        done(whole.at[0, 0], rsem.at[7 * NCH + h])
        late = pltpu.make_async_copy(whole.at[1 - core, h], grads_h.at[1 - core, h], osem.at[4 + h])
        late.start()
        stores.append(late)

    for h in range(NCH):
        done(others(send_z, groups), fsem.at[h])
        done(others(send_m, members), fsem.at[NCH + h])
        done(others(back_m, members), fsem.at[2 * NCH + h])
        done(others(back_z, groups), fsem.at[3 * NCH + h])
        done(x_recv.at[h], ssem.at[NCH + h])
        done(y_recv.at[h], ssem.at[2 * NCH + h])
        done(z_recv.at[h, pl.ds(0, near - 1)], ssem.at[3 * NCH + h])
        done(z_last.at[h, pl.ds(0, runs - 1)], ssem.at[4 * NCH + h])
        done(whole.at[0, 0, pl.ds(0, (ny - 1) * piece)], ssem.at[5 * NCH + h])
        done(whole.at[0, 0, pl.ds(0, (nx - 1) * chunk)], ssem.at[6 * NCH + h])
        done(whole.at[0, 0], ssem.at[7 * NCH + h])
    done(bias_x.at[pl.ds(0, nx - 1)], ssem.at[bias_sem + 1])
    done(bias_y.at[pl.ds(0, ny - 1)], ssem.at[bias_sem + 2])
    done(bias_z.at[pl.ds(0, near - 1)], ssem.at[bias_sem + 3])
    done(bias_zl.at[pl.ds(0, runs - 1)], ssem.at[bias_sem + 4])
    for store in stores:
        store.wait()


def finish(out_v, gfeat_v, grads_v, gbias_v, out, gfeat, gws, gwn, gbias, rows, low, full, line, sem):
    wide = grads_v.shape[3]
    parts = [(i, h) for i in range(2) for h in range(NCH)]
    loads = [
        (out_v, rows.at[0]), (gfeat_v, rows.at[1]), (gbias_v, line),
        *((grads_v.at[i, h], low.at[i, h]) for i, h in parts),
    ]
    stores = [(rows.at[0], out), (rows.at[1], gfeat), (line, gbias), (full.at[0], gws), (full.at[1], gwn)]
    loads = [pltpu.make_async_copy(a, b, sem.at[i]) for i, (a, b) in enumerate(loads)]
    stores = [pltpu.make_async_copy(a, b, sem.at[len(loads) + i]) for i, (a, b) in enumerate(stores)]
    for load in loads:
        load.start()
    for i in range(3):
        loads[i].wait()
        stores[i].start()
    for k, (i, h) in enumerate(parts):
        loads[3 + k].wait()
        full[i, :, h * wide:(h + 1) * wide] = low[i, h].astype(F32)
        if h == NCH - 1:
            stores[3 + i].start()
    for store in stores:
        store.wait()


def shards(
    nx, features, w_self, w_neigh, bias, set_members, set_size, cross_list, inner_list,
    ref_slot, ref_count, cotangent,
):
    nodes, width = features.shape
    sets, most = set_members.shape
    groups = lax.axis_size("group")
    members = lax.axis_size("member")
    refs = ref_slot.shape[1]
    cap = cross_list.shape[3]
    ny, nz = members // nx, groups // CORES
    near = z_near(nz)
    chunk = width // nx
    piece = chunk // ny
    wide = width // NCH
    relays, slots = groups * cap, members * cap
    V = pltpu.VMEM
    S = jax.ShapeDtypeStruct
    outs = pl.pallas_call(
        functools.partial(kernel, groups, members, nx, cap),
        out_shape=(
            S((nodes, width), BF), S((nodes, width), BF), S((2, NCH, width, wide), BF), S((1, width), F32),
        ),
        in_specs=[pl.BlockSpec(memory_space=pl.ANY)] * 11,
        out_specs=(pl.BlockSpec(memory_space=pl.ANY),) * 4,
        scratch_shapes=[
            V((nodes, width), BF), V((width, width), BF), V((width, width), BF), V((1, width), F32),
            V((most, sets), I32), V((1, sets), I32), V((cap, groups), I32), V((cap, members), I32),
            V((refs, nodes), I32), V((1, nodes), I32), V((nodes, width), BF),
            V((nodes, sets), BF), V((sets, nodes), BF),
            V((slots, nodes), BF), V((nodes, slots), BF),
            V((sets, relays), BF), V((relays, sets), BF),
            V((relays, slots), BF), V((slots, relays), BF),
            V((width, nodes), BF), V((nodes, 128), F32),
            V((NCH, relays, wide), BF), V((NCH, relays, wide), BF),
            V((NCH, slots, wide), BF), V((NCH, slots, wide), BF),
            V((nodes, width), BF), V((nodes, width), BF),
            V((nodes, width), F32), V((nodes, width), F32),
            V((2, nodes, wide), BF),
            V((NCH, slots, wide), BF), V((NCH, slots, wide), BF),
            V((NCH, relays, wide), BF), V((NCH, relays, wide), BF),
            V((width, nodes), BF), V((2, NCH, width, wide), F32),
            V((NCH, width, wide), BF), V((NCH, width, wide), BF), V((NCH, width, wide), BF),
            V((NCH, nx - 1, chunk, wide), BF), V((NCH, chunk, wide), F32), V((NCH, chunk, wide), BF),
            V((NCH, ny - 1, piece, wide), BF), V((NCH, near, piece, wide), BF), V((NCH, nz // near, piece, wide), BF),
            V((2, NCH, width, wide), BF),
            V((nodes, width), BF), V((nodes, width), BF), V((1, width), F32),
            V((8, 128), F32), V((8, 128), F32), V((nx, 8, 128), F32), V((ny, 8, 128), F32),
            V((near, 8, 128), F32), V((nz // near, 8, 128), F32),
            pltpu.SemaphoreType.DMA((11,)),
            pltpu.SemaphoreType.DMA((4 + NCH,)),
            pltpu.SemaphoreType.DMA((8 * NCH + 5,)),
            pltpu.SemaphoreType.DMA((8 * NCH + 5,)),
            pltpu.SemaphoreType.DMA((4 * NCH,)),
            pltpu.SemaphoreType.DMA((4 * NCH,)),
        ],
        compiler_params=pltpu.CompilerParams(
            collective_id=0, has_side_effects=True, vmem_limit_bytes=60 * 2**20
        ),
    )(
        features, w_self, w_neigh, bias.reshape(1, width), set_members.T, set_size.reshape(1, sets),
        cross_list[0, 0].T, inner_list[0, 0].T, ref_slot.T, ref_count.reshape(1, nodes), cotangent,
    )
    anywhere = pl.BlockSpec(memory_space=pl.ANY)
    output, gfeat, gws, gwn, gbias = pl.pallas_call(
        finish,
        out_shape=(
            S((nodes, width), BF), S((nodes, width), BF), S((width, width), F32), S((width, width), F32),
            S((1, width), F32),
        ),
        in_specs=[anywhere] * 4,
        out_specs=(anywhere,) * 5,
        scratch_shapes=[
            V((2, nodes, width), BF), V((2, NCH, width, wide), BF), V((2, width, width), F32), V((1, width), F32),
            pltpu.SemaphoreType.DMA((8 + 2 * NCH,)),
        ],
        compiler_params=pltpu.CompilerParams(vmem_limit_bytes=60 * 2**20),
    )(*outs)
    return output, gfeat, gws, gwn, gbias.reshape(width)


def solution(mesh):
    nx = 4
    in_specs = (
        P(("group", "member"), None),
        P(),
        P(),
        P(),
        P(("group", "member"), None),
        P(("group", "member")),
        P("group", "member", None, None),
        P("group", "member", None, None),
        P(("group", "member"), None),
        P(("group", "member")),
        P(("group", "member"), None),
    )
    out_specs = (P(("group", "member"), None), P(("group", "member"), None), P(), P(), P())
    return jax.shard_map(
        functools.partial(shards, nx), mesh=mesh, in_specs=in_specs, out_specs=out_specs, check_vma=False
    )
```

```python
import functools

import jax
import jax.numpy as jnp
from jax import lax
from jax.experimental import pallas as pl
from jax.experimental.pallas import tpu as pltpu
from jax.sharding import PartitionSpec as P

MESH = pl.DeviceIdType.MESH
BF = jnp.bfloat16
F32 = jnp.float32
I32 = jnp.int32
CORES = 2
FCH = 4
BCH = 4
ACH = 2


def dot(a, b, ca=1, cb=0):
    return lax.dot_general(a, b, (((ca,), (cb,)), ((), ())), preferred_element_type=F32)


def iota(shape, dim):
    return lax.broadcasted_iota(I32, shape, dim)


def flat_row(table):
    cap, n = table.shape
    expand = jnp.where(iota((n, n * cap), 1) // cap == iota((n, n * cap), 0), 1.0, 0.0).astype(BF)
    high = dot((table // 16).astype(F32).astype(BF), expand)
    low = dot((table % 16).astype(F32).astype(BF), expand)
    keep = iota((cap, n * cap), 1) % cap == iota((cap, n * cap), 0)
    return jnp.sum(jnp.where(keep, high * 16.0 + low, 0.0), axis=0, keepdims=True).astype(I32)


def hits(table, count, first, rows):
    entries, n = table.shape
    live = jnp.where(iota((entries, n), 0) < count, table, -1)
    sub = iota((rows, n), 0) + first
    acc = jnp.zeros((rows, n), F32)
    for k in range(entries):
        acc += jnp.where(live[k:k + 1, :] == sub, 1.0, 0.0)
    return acc.astype(BF)


def z_near(nz):
    return 4 if nz % 4 == 0 else nz


def kernel(
    groups, members, nx, cap,
    feats_h, w_self_h, w_neigh_h, bias_h, mem_h, size_h, cross_h, inner_h, ref_h, count_h, cot_h,
    out_h, gfeat_h, grads_h, gbias_h,
    feats, w_self, w_neigh, bias, mem, size, cross, inner, ref, count, cot,
    member_t, member_n, ref_t, ref_n, cross_t, cross_n, inner_t, inner_n, left, inv,
    send_z, relay, send_m, arrived,
    neigh, low, pre, own, split, back_m, returned, back_z, homeward,
    part, core_send, core_recv, x_send, x_recv, y_full, y_send, y_recv, z_recv, z_last, whole,
    out, gfeat, gbias,
    bias_own, bias_core, bias_x, bias_y, bias_z, bias_zl,
    lsem, osem, ssem, rsem, fsem, gsem,
):
    g = lax.axis_index("group")
    m = lax.axis_index("member")
    z, core = g // CORES, g % CORES
    y, x = m // nx, m % nx
    nz, ny = groups // CORES, members // nx
    near = z_near(nz)
    runs = nz // near
    nodes, width = feats.shape
    sets = mem.shape[1]
    fwide, bwide, awide = width // FCH, width // BCH, width // ACH
    relays, slots = groups * cap, members * cap
    pairs = (
        (mem_h, mem), (size_h, size), (cross_h, cross), (feats_h, feats), (inner_h, inner), (ref_h, ref),
        (count_h, count), (w_self_h, w_self), (bias_h, bias), (w_neigh_h, w_neigh), (cot_h, cot),
    )
    loads = [pltpu.make_async_copy(a, b, lsem.at[i]) for i, (a, b) in enumerate(pairs)]
    for load in loads:
        load.start()

    barrier = pltpu.get_barrier_semaphore()

    def around(count, me, go):
        def body(k, c):
            s = (k + 1) // 2
            go(lax.rem(jnp.where(k % 2 == 1, me + s, me - s + count), count))
            return c
        lax.fori_loop(1, count, body, 0)

    def greet(axis, count, me):
        def go(peer):
            pl.semaphore_signal(barrier, inc=1, device_id={axis: peer}, device_id_type=MESH)
        around(count, me, go)

    greet("group", groups, g)
    greet("member", members, m)

    def remote(src, dst, sems, which, target):
        return pltpu.make_async_remote_copy(
            src_ref=src, dst_ref=dst, send_sem=sems[0].at[which], recv_sem=sems[1].at[which],
            device_id=target, device_id_type=MESH,
        )

    def done(ref, sem):
        pltpu.make_async_copy(ref, ref, sem).wait()

    rows_sems = (fsem, gsem)

    def exchange(src, dst, which, axis, count, me):
        def go(peer):
            at = pl.multiple_of(peer * cap, cap)
            to = pl.multiple_of(me * cap, cap)
            remote(src.at[pl.ds(at, cap)], dst.at[pl.ds(to, cap)], rows_sems, which, {axis: peer}).start()
        around(count, me, go)
        mine = pl.ds(pl.multiple_of(me * cap, cap), cap)
        dst[mine, :] = src[mine, :]

    def others(buf, count):
        return buf.at[0, pl.ds(0, (count - 1) * cap)]

    blk = 64
    loads[0].wait()
    loads[1].wait()
    for b in range(nodes // blk):
        member_t[b * blk:(b + 1) * blk, :] = hits(mem[...], size[...], b * blk, blk)
    member_n[...] = member_t[...].T
    loads[2].wait()
    cross_t[...] = jnp.where(flat_row(cross[...]) == iota((sets, relays), 0), 1.0, 0.0).astype(BF)
    cross_n[...] = cross_t[...].T
    loads[3].wait()
    for h in range(FCH):
        cols = slice(h * fwide, (h + 1) * fwide)
        agg = dot(member_n[...], feats[:, cols]).astype(BF)
        send_z[h] = dot(cross_n[...], agg).astype(BF)
        if h == 0:
            pl.semaphore_wait(barrier, groups + members - 2)
        exchange(send_z.at[h], relay.at[h], h, "group", groups, g)

    loads[4].wait()
    inner_t[...] = jnp.where(flat_row(inner[...]) == iota((relays, slots), 0), 1.0, 0.0).astype(BF)
    inner_n[...] = inner_t[...].T
    loads[5].wait()
    loads[6].wait()
    blk = 32
    for b in range(slots // blk):
        ref_t[b * blk:(b + 1) * blk, :] = hits(ref[...], count[...], b * blk, blk)
    ref_n[...] = ref_t[...].T
    inv[...] = jnp.broadcast_to(1.0 / count[...].astype(F32), (128, nodes)).T
    left[0] = feats[...].T
    loads[7].wait()
    loads[8].wait()
    pre[...] = dot(feats[...], w_self[...]) + bias[...]
    loads[9].wait()
    loads[10].wait()

    for h in range(FCH):
        done(others(relay, groups), gsem.at[h])
        send_m[h] = dot(inner_n[...], relay[h]).astype(BF)
        exchange(send_m.at[h], arrived.at[h], FCH + h, "member", members, m)

    blk = 128
    for h in range(FCH):
        done(others(arrived, members), gsem.at[FCH + h])
        cols = slice(h * fwide, (h + 1) * fwide)
        for b in range(nodes // blk):
            rows = slice(b * blk, (b + 1) * blk)
            mean = (dot(ref_n[rows, :], arrived[h]) * inv[rows, 0:1]).astype(BF)
            neigh[rows, cols] = mean
            if h < FCH - 1:
                pre[rows, :] += dot(mean, w_neigh[cols, :])
        left[1, cols, :] = neigh[:, cols].T

    sums = (ssem, rsem)
    chunk = width // nx
    piece = chunk // ny
    sibling = {"group": z * CORES + 1 - core}
    x_rows = pl.ds(pl.multiple_of(x * chunk, chunk), chunk)
    y_rows = pl.ds(pl.multiple_of(y * piece, piece), piece)
    piece_rows = pl.ds(pl.multiple_of(x * chunk + y * piece, piece), piece)
    spot, run = z % near, z // near
    bias_sem = 8 * ACH
    bias_own[...] = jnp.zeros_like(bias_own)

    def ring(me, count, k):
        return lax.rem(me + k, count)

    def x_target(p):
        return {"member": y * nx + p}

    def y_target(p):
        return {"member": p * nx + x}

    def z_target(p):
        return {"group": p * CORES + core}

    def add_up(buf, n, first=None):
        acc = buf[0].astype(F32) if first is None else first + buf[0].astype(F32)
        for i in range(1, n):
            acc += buf[i].astype(F32)
        return acc

    def core_copy(h):
        return remote(core_send.at[h], core_recv.at[h], sums, h, sibling)

    def bias_copy():
        return remote(bias_own, bias_core, sums, bias_sem, sibling)

    def layer(h):
        cols = slice(h * awide, (h + 1) * awide)
        late = slice((FCH - 1) * fwide, width)
        total = jnp.zeros((1, awide), F32)
        for b in range(nodes // blk):
            rows = slice(b * blk, (b + 1) * blk)
            p = pre[rows, cols] + dot(neigh[rows, late], w_neigh[late, cols])
            gate = jax.nn.sigmoid(p)
            out[rows, cols] = (p * gate).astype(BF)
            full = cot[rows, cols].astype(F32) * gate * (1.0 + p * (1.0 - gate))
            total = total + jnp.sum(full, axis=0, keepdims=True)
            low[rows, cols] = full.astype(BF)
        for i in range(awide // 128):
            at = h * (awide // 128) + i
            bias_own[at:at + 1, :] = total[:, i * 128:(i + 1) * 128]

    def core_stage(h):
        cols = slice(h * awide, (h + 1) * awide)
        layer(h)
        core_send[h] = dot(left[1 - core], low[:, cols]).astype(BF)
        core_copy(h).start()
        part[h] = dot(left[core], low[:, cols])
        if h == ACH - 1:
            bias_copy().start()

    def x_stage(h):
        core_copy(h).wait()
        total = part[h] + core_recv[h].astype(F32)
        part[h] = total
        x_send[h] = total.astype(BF)
        for k in range(1, nx):
            p = ring(x, nx, k)
            at = pl.ds(pl.multiple_of(p * chunk, chunk), chunk)
            remote(x_send.at[h, at], x_recv.at[h, k - 1], sums, ACH + h, x_target(p)).start()
        if h == ACH - 1:
            bias_copy().wait()
            bias_x[x] = bias_own[...] + bias_core[...]
            for k in range(1, nx):
                p = ring(x, nx, k)
                remote(bias_x.at[x], bias_x.at[x], sums, bias_sem + 1, x_target(p)).start()

    def y_stage(h):
        done(x_recv.at[h], rsem.at[ACH + h])
        total = add_up(x_recv.at[h], nx - 1, part[h, x_rows, :])
        y_full[h] = total
        y_send[h] = total.astype(BF)
        for k in range(1, ny):
            p = ring(y, ny, k)
            at = pl.ds(pl.multiple_of(p * piece, piece), piece)
            remote(y_send.at[h, at], y_recv.at[h, k - 1], sums, 2 * ACH + h, y_target(p)).start()
        if h == ACH - 1:
            done(bias_x.at[pl.ds(0, nx - 1)], rsem.at[bias_sem + 1])
            bias_y[y] = add_up(bias_x, nx)
            for k in range(1, ny):
                p = ring(y, ny, k)
                remote(bias_y.at[y], bias_y.at[y], sums, bias_sem + 2, y_target(p)).start()

    def z_stage(h):
        done(y_recv.at[h], rsem.at[2 * ACH + h])
        z_recv[h, spot] = add_up(y_recv.at[h], ny - 1, y_full[h, y_rows, :]).astype(BF)
        for k in range(1, near):
            p = run * near + ring(spot, near, k)
            remote(z_recv.at[h, spot], z_recv.at[h, spot], sums, 3 * ACH + h, z_target(p)).start()
        if h == ACH - 1:
            done(bias_y.at[pl.ds(0, ny - 1)], rsem.at[bias_sem + 2])
            bias_z[spot] = add_up(bias_y, ny)
            for k in range(1, near):
                p = run * near + ring(spot, near, k)
                remote(bias_z.at[spot], bias_z.at[spot], sums, bias_sem + 3, z_target(p)).start()

    def z_next(h):
        done(z_recv.at[h, pl.ds(0, near - 1)], rsem.at[3 * ACH + h])
        z_last[h, run] = add_up(z_recv.at[h], near).astype(BF)
        for k in range(1, runs):
            p = ring(run, runs, k) * near + spot
            remote(z_last.at[h, run], z_last.at[h, run], sums, 4 * ACH + h, z_target(p)).start()
        if h == ACH - 1:
            done(bias_z.at[pl.ds(0, near - 1)], rsem.at[bias_sem + 3])
            bias_zl[run] = add_up(bias_z, near)
            for k in range(1, runs):
                p = ring(run, runs, k) * near + spot
                remote(bias_zl.at[run], bias_zl.at[run], sums, bias_sem + 4, z_target(p)).start()

    def y_back(h):
        done(z_last.at[h, pl.ds(0, runs - 1)], rsem.at[4 * ACH + h])
        whole[core, h, piece_rows, :] = add_up(z_last.at[h], runs).astype(BF)
        at = whole.at[core, h, piece_rows]
        for k in range(1, ny):
            remote(at, at, sums, 5 * ACH + h, y_target(ring(y, ny, k))).start()

    def x_back(h):
        done(whole.at[0, 0, pl.ds(0, (ny - 1) * piece)], rsem.at[5 * ACH + h])
        at = whole.at[core, h, x_rows]
        for k in range(1, nx):
            remote(at, at, sums, 6 * ACH + h, x_target(ring(x, nx, k))).start()

    def core_back(h):
        done(whole.at[0, 0, pl.ds(0, (nx - 1) * chunk)], rsem.at[6 * ACH + h])
        remote(whole.at[core, h], whole.at[core, h], sums, 7 * ACH + h, sibling).start()

    def member_back(h):
        cols = slice(h * bwide, (h + 1) * bwide)
        for b in range(nodes // blk):
            rows = slice(b * blk, (b + 1) * blk)
            gn = dot(low[rows, :], w_neigh[cols, :], 1, 1) * inv[rows, 0:1]
            hi = gn.astype(BF)
            split[0, rows, :] = hi
            split[1, rows, :] = (gn - hi.astype(F32)).astype(BF)
        back_m[h] = (dot(ref_t[...], split[0]) + dot(ref_t[...], split[1])).astype(BF)

    def member_send(h):
        exchange(back_m.at[h], returned.at[h], 2 * FCH + h, "member", members, m)

    def home(h):
        done(others(returned, members), gsem.at[2 * FCH + h])
        back_z[h] = dot(inner_t[...], returned[h]).astype(BF)
        exchange(back_z.at[h], homeward.at[h], 2 * FCH + BCH + h, "group", groups, g)

    def features_back(h):
        cols = slice(h * bwide, (h + 1) * bwide)
        done(others(homeward, groups), gsem.at[2 * FCH + BCH + h])
        grad_agg = dot(cross_t[...], homeward[h]).astype(BF)
        gfeat[:, cols] = (own[:, cols] + dot(member_t[...], grad_agg)).astype(BF)

    stores = [
        pltpu.make_async_copy(out, out_h, osem.at[0]),
        pltpu.make_async_copy(gfeat, gfeat_h, osem.at[1]),
        pltpu.make_async_copy(gbias, gbias_h, osem.at[2]),
        pltpu.make_async_copy(whole.at[core], grads_h.at[core], osem.at[3]),
    ]
    core_stage(0)
    core_stage(1)
    stores[0].start()
    member_back(0)
    member_back(1)
    x_stage(0)
    member_back(2)
    member_back(3)
    x_stage(1)
    own[...] = dot(low[...], w_self[...], 1, 1)
    y_stage(0)
    y_stage(1)
    member_send(0)
    member_send(1)
    member_send(2)
    member_send(3)
    z_stage(0)
    z_stage(1)
    z_next(0)
    z_next(1)
    home(0)
    home(1)
    y_back(0)
    home(2)
    y_back(1)
    home(3)
    x_back(0)
    x_back(1)
    features_back(0)
    features_back(1)
    features_back(2)
    core_back(0)
    features_back(3)
    core_back(1)
    done(bias_zl.at[pl.ds(0, runs - 1)], rsem.at[bias_sem + 4])
    bias_sum = add_up(bias_zl, runs)
    for i in range(width // 128):
        gbias[:, i * 128:(i + 1) * 128] = bias_sum[i:i + 1, :]
    for store in stores[1:]:
        store.start()
    for h in range(ACH):
        done(whole.at[0, 0], rsem.at[7 * ACH + h])
        late = pltpu.make_async_copy(whole.at[1 - core, h], grads_h.at[1 - core, h], osem.at[4 + h])
        late.start()
        stores.append(late)

    for h in range(FCH):
        done(others(send_z, groups), fsem.at[h])
        done(others(send_m, members), fsem.at[FCH + h])
    for h in range(BCH):
        done(others(back_m, members), fsem.at[2 * FCH + h])
        done(others(back_z, groups), fsem.at[2 * FCH + BCH + h])
    for h in range(ACH):
        done(x_recv.at[h], ssem.at[ACH + h])
        done(y_recv.at[h], ssem.at[2 * ACH + h])
        done(z_recv.at[h, pl.ds(0, near - 1)], ssem.at[3 * ACH + h])
        done(z_last.at[h, pl.ds(0, runs - 1)], ssem.at[4 * ACH + h])
        done(whole.at[0, 0, pl.ds(0, (ny - 1) * piece)], ssem.at[5 * ACH + h])
        done(whole.at[0, 0, pl.ds(0, (nx - 1) * chunk)], ssem.at[6 * ACH + h])
        done(whole.at[0, 0], ssem.at[7 * ACH + h])
    done(bias_x.at[pl.ds(0, nx - 1)], ssem.at[bias_sem + 1])
    done(bias_y.at[pl.ds(0, ny - 1)], ssem.at[bias_sem + 2])
    done(bias_z.at[pl.ds(0, near - 1)], ssem.at[bias_sem + 3])
    done(bias_zl.at[pl.ds(0, runs - 1)], ssem.at[bias_sem + 4])
    for store in stores:
        store.wait()


def finish(out_v, gfeat_v, grads_v, gbias_v, out, gfeat, gws, gwn, gbias, rows, low, full, line, sem):
    wide = grads_v.shape[3]
    parts = [(i, h) for i in range(2) for h in range(ACH)]
    loads = [
        *((grads_v.at[i, h], low.at[i, h]) for i, h in parts),
        (out_v, rows.at[0]), (gfeat_v, rows.at[1]), (gbias_v, line),
    ]
    stores = [
        *((full.at[i, h], (gws, gwn)[i].at[:, pl.ds(h * wide, wide)]) for i, h in parts),
        (rows.at[0], out), (rows.at[1], gfeat), (line, gbias),
    ]
    loads = [pltpu.make_async_copy(a, b, sem.at[i]) for i, (a, b) in enumerate(loads)]
    stores = [pltpu.make_async_copy(a, b, sem.at[len(loads) + i]) for i, (a, b) in enumerate(stores)]
    for load in loads:
        load.start()
    for k, (load, store) in enumerate(zip(loads, stores)):
        load.wait()
        if k < len(parts):
            i, h = parts[k]
            full[i, h] = low[i, h].astype(F32)
        store.start()
    for store in stores:
        store.wait()


def shards(
    nx, features, w_self, w_neigh, bias, set_members, set_size, cross_list, inner_list,
    ref_slot, ref_count, cotangent,
):
    nodes, width = features.shape
    sets, most = set_members.shape
    groups = lax.axis_size("group")
    members = lax.axis_size("member")
    refs = ref_slot.shape[1]
    cap = cross_list.shape[3]
    ny, nz = members // nx, groups // CORES
    near = z_near(nz)
    chunk = width // nx
    piece = chunk // ny
    fwide, bwide, awide = width // FCH, width // BCH, width // ACH
    relays, slots = groups * cap, members * cap
    V = pltpu.VMEM
    S = jax.ShapeDtypeStruct
    outs = pl.pallas_call(
        functools.partial(kernel, groups, members, nx, cap),
        out_shape=(
            S((nodes, width), BF), S((nodes, width), BF), S((2, ACH, width, awide), BF), S((1, width), F32),
        ),
        in_specs=[pl.BlockSpec(memory_space=pl.ANY)] * 11,
        out_specs=(pl.BlockSpec(memory_space=pl.ANY),) * 4,
        scratch_shapes=[
            V((nodes, width), BF), V((width, width), BF), V((width, width), BF), V((1, width), F32),
            V((most, sets), I32), V((1, sets), I32), V((cap, groups), I32), V((cap, members), I32),
            V((refs, nodes), I32), V((1, nodes), I32), V((nodes, width), BF),
            V((nodes, sets), BF), V((sets, nodes), BF),
            V((slots, nodes), BF), V((nodes, slots), BF),
            V((sets, relays), BF), V((relays, sets), BF),
            V((relays, slots), BF), V((slots, relays), BF),
            V((2, width, nodes), BF), V((nodes, 128), F32),
            V((FCH, relays, fwide), BF), V((FCH, relays, fwide), BF),
            V((FCH, slots, fwide), BF), V((FCH, slots, fwide), BF),
            V((nodes, width), BF), V((nodes, width), BF),
            V((nodes, width), F32), V((nodes, width), F32),
            V((2, nodes, bwide), BF),
            V((BCH, slots, bwide), BF), V((BCH, slots, bwide), BF),
            V((BCH, relays, bwide), BF), V((BCH, relays, bwide), BF),
            V((ACH, width, awide), F32),
            V((ACH, width, awide), BF), V((ACH, width, awide), BF), V((ACH, width, awide), BF),
            V((ACH, nx - 1, chunk, awide), BF), V((ACH, chunk, awide), F32), V((ACH, chunk, awide), BF),
            V((ACH, ny - 1, piece, awide), BF), V((ACH, near, piece, awide), BF), V((ACH, nz // near, piece, awide), BF),
            V((2, ACH, width, awide), BF),
            V((nodes, width), BF), V((nodes, width), BF), V((1, width), F32),
            V((8, 128), F32), V((8, 128), F32), V((nx, 8, 128), F32), V((ny, 8, 128), F32),
            V((near, 8, 128), F32), V((nz // near, 8, 128), F32),
            pltpu.SemaphoreType.DMA((11,)),
            pltpu.SemaphoreType.DMA((4 + ACH,)),
            pltpu.SemaphoreType.DMA((8 * ACH + 5,)),
            pltpu.SemaphoreType.DMA((8 * ACH + 5,)),
            pltpu.SemaphoreType.DMA((2 * FCH + 2 * BCH,)),
            pltpu.SemaphoreType.DMA((2 * FCH + 2 * BCH,)),
        ],
        compiler_params=pltpu.CompilerParams(
            collective_id=0, has_side_effects=True, vmem_limit_bytes=60 * 2**20
        ),
    )(
        features, w_self, w_neigh, bias.reshape(1, width), set_members.T, set_size.reshape(1, sets),
        cross_list[0, 0].T, inner_list[0, 0].T, ref_slot.T, ref_count.reshape(1, nodes), cotangent,
    )
    anywhere = pl.BlockSpec(memory_space=pl.ANY)
    output, gfeat, gws, gwn, gbias = pl.pallas_call(
        finish,
        out_shape=(
            S((nodes, width), BF), S((nodes, width), BF), S((width, width), F32), S((width, width), F32),
            S((1, width), F32),
        ),
        in_specs=[anywhere] * 4,
        out_specs=(anywhere,) * 5,
        scratch_shapes=[
            V((2, nodes, width), BF), V((2, ACH, width, awide), BF), V((2, ACH, width, awide), F32), V((1, width), F32),
            pltpu.SemaphoreType.DMA((6 + 4 * ACH,)),
        ],
        compiler_params=pltpu.CompilerParams(vmem_limit_bytes=60 * 2**20),
    )(*outs)
    return output, gfeat, gws, gwn, gbias.reshape(width)


def solution(mesh):
    nx = 4
    in_specs = (
        P(("group", "member"), None),
        P(),
        P(),
        P(),
        P(("group", "member"), None),
        P(("group", "member")),
        P("group", "member", None, None),
        P("group", "member", None, None),
        P(("group", "member"), None),
        P(("group", "member")),
        P(("group", "member"), None),
    )
    out_specs = (P(("group", "member"), None), P(("group", "member"), None), P(), P(), P())
    return jax.shard_map(
        functools.partial(shards, nx), mesh=mesh, in_specs=in_specs, out_specs=out_specs, check_vma=False
    )
```

```python
import functools

import jax
import jax.numpy as jnp
from jax import lax
from jax.experimental import pallas as pl
from jax.experimental.pallas import tpu as pltpu
from jax.sharding import PartitionSpec as P

MESH = pl.DeviceIdType.MESH
BF = jnp.bfloat16
F32 = jnp.float32
I32 = jnp.int32
CORES = 2
FCH = 4
BCH = 4
ACH = 2


def dot(a, b, ca=1, cb=0):
    return lax.dot_general(a, b, (((ca,), (cb,)), ((), ())), preferred_element_type=F32)


def iota(shape, dim):
    return lax.broadcasted_iota(I32, shape, dim)


def flat_row(table):
    cap, n = table.shape
    expand = jnp.where(iota((n, n * cap), 1) // cap == iota((n, n * cap), 0), 1.0, 0.0).astype(BF)
    high = dot((table // 16).astype(F32).astype(BF), expand)
    low = dot((table % 16).astype(F32).astype(BF), expand)
    keep = iota((cap, n * cap), 1) % cap == iota((cap, n * cap), 0)
    return jnp.sum(jnp.where(keep, high * 16.0 + low, 0.0), axis=0, keepdims=True).astype(I32)


def hits(table, count, first, rows):
    entries, n = table.shape
    live = jnp.where(iota((entries, n), 0) < count, table, -1)
    sub = iota((rows, n), 0) + first
    acc = jnp.zeros((rows, n), F32)
    for k in range(entries):
        acc += jnp.where(live[k:k + 1, :] == sub, 1.0, 0.0)
    return acc.astype(BF)


def z_near(nz):
    return 4 if nz % 4 == 0 else nz


def kernel(
    groups, members, nx, cap,
    feats_h, w_self_h, w_neigh_h, bias_h, mem_h, size_h, cross_h, inner_h, ref_h, count_h, cot_h,
    out_h, gfeat_h, grads_h, gbias_h,
    feats, w_self, w_neigh, bias, mem, size, cross, inner, ref, count, cot,
    member_t, member_n, ref_t, ref_n, cross_t, cross_n, inner_t, inner_n, left, inv,
    send_z, relay, send_m, arrived,
    neigh, low, pre, own, split, back_m, returned, back_z, homeward,
    part, core_send, core_recv, x_send, x_recv, y_full, y_send, y_recv, z_recv, z_last, whole,
    out, gfeat, gbias,
    bias_own, bias_core, bias_x, bias_y, bias_z, bias_zl,
    lsem, osem, ssem, rsem, fsem, gsem,
):
    g = lax.axis_index("group")
    m = lax.axis_index("member")
    z, core = g // CORES, g % CORES
    y, x = m // nx, m % nx
    nz, ny = groups // CORES, members // nx
    near = z_near(nz)
    runs = nz // near
    nodes, width = feats.shape
    sets = mem.shape[1]
    fwide, bwide, awide = width // FCH, width // BCH, width // ACH
    relays, slots = groups * cap, members * cap
    pairs = (
        (mem_h, mem), (size_h, size), (cross_h, cross), (feats_h, feats), (inner_h, inner), (ref_h, ref),
        (count_h, count), (w_self_h, w_self), (bias_h, bias), (w_neigh_h, w_neigh), (cot_h, cot),
    )
    loads = [pltpu.make_async_copy(a, b, lsem.at[i]) for i, (a, b) in enumerate(pairs)]
    for load in loads:
        load.start()

    barrier = pltpu.get_barrier_semaphore()

    def around(count, me, go):
        def body(k, c):
            s = (k + 1) // 2
            go(lax.rem(jnp.where(k % 2 == 1, me + s, me - s + count), count))
            return c
        lax.fori_loop(1, count, body, 0)

    def greet(axis, count, me):
        def go(peer):
            pl.semaphore_signal(barrier, inc=1, device_id={axis: peer}, device_id_type=MESH)
        around(count, me, go)

    greet("group", groups, g)
    greet("member", members, m)

    def remote(src, dst, sems, which, target):
        return pltpu.make_async_remote_copy(
            src_ref=src, dst_ref=dst, send_sem=sems[0].at[which], recv_sem=sems[1].at[which],
            device_id=target, device_id_type=MESH,
        )

    def done(ref, sem):
        pltpu.make_async_copy(ref, ref, sem).wait()

    rows_sems = (fsem, gsem)

    def exchange(src, dst, which, axis, count, me):
        def go(peer):
            at = pl.multiple_of(peer * cap, cap)
            to = pl.multiple_of(me * cap, cap)
            remote(src.at[pl.ds(at, cap)], dst.at[pl.ds(to, cap)], rows_sems, which, {axis: peer}).start()
        around(count, me, go)
        mine = pl.ds(pl.multiple_of(me * cap, cap), cap)
        dst[mine, :] = src[mine, :]

    def others(buf, count):
        return buf.at[0, pl.ds(0, (count - 1) * cap)]

    blk = 64
    loads[0].wait()
    loads[1].wait()
    for b in range(nodes // blk):
        member_t[b * blk:(b + 1) * blk, :] = hits(mem[...], size[...], b * blk, blk)
    member_n[...] = member_t[...].T
    loads[2].wait()
    cross_t[...] = jnp.where(flat_row(cross[...]) == iota((sets, relays), 0), 1.0, 0.0).astype(BF)
    cross_n[...] = cross_t[...].T
    loads[3].wait()
    for h in range(FCH):
        cols = slice(h * fwide, (h + 1) * fwide)
        agg = dot(member_n[...], feats[:, cols]).astype(BF)
        send_z[h] = dot(cross_n[...], agg).astype(BF)
        if h == 0:
            pl.semaphore_wait(barrier, groups + members - 2)
        exchange(send_z.at[h], relay.at[h], h, "group", groups, g)

    loads[4].wait()
    inner_t[...] = jnp.where(flat_row(inner[...]) == iota((relays, slots), 0), 1.0, 0.0).astype(BF)
    inner_n[...] = inner_t[...].T
    loads[5].wait()
    loads[6].wait()
    blk = 32
    for b in range(slots // blk):
        ref_t[b * blk:(b + 1) * blk, :] = hits(ref[...], count[...], b * blk, blk)
    ref_n[...] = ref_t[...].T
    inv[...] = jnp.broadcast_to(1.0 / count[...].astype(F32), (128, nodes)).T
    left[0] = feats[...].T
    loads[7].wait()
    loads[8].wait()
    pre[...] = dot(feats[...], w_self[...]) + bias[...]
    loads[9].wait()
    loads[10].wait()

    for h in range(FCH):
        done(others(relay, groups), gsem.at[h])
        send_m[h] = dot(inner_n[...], relay[h]).astype(BF)
        exchange(send_m.at[h], arrived.at[h], FCH + h, "member", members, m)

    blk = 128
    for h in range(FCH):
        done(others(arrived, members), gsem.at[FCH + h])
        cols = slice(h * fwide, (h + 1) * fwide)
        for b in range(nodes // blk):
            rows = slice(b * blk, (b + 1) * blk)
            mean = (dot(ref_n[rows, :], arrived[h]) * inv[rows, 0:1]).astype(BF)
            neigh[rows, cols] = mean
            if h < FCH - 1:
                pre[rows, :] += dot(mean, w_neigh[cols, :])
        left[1, cols, :] = neigh[:, cols].T

    sums = (ssem, rsem)
    chunk = width // nx
    piece = chunk // ny
    sibling = {"group": z * CORES + 1 - core}
    x_rows = pl.ds(pl.multiple_of(x * chunk, chunk), chunk)
    y_rows = pl.ds(pl.multiple_of(y * piece, piece), piece)
    piece_rows = pl.ds(pl.multiple_of(x * chunk + y * piece, piece), piece)
    spot, run = z % near, z // near
    bias_sem = 8 * ACH
    bias_own[...] = jnp.zeros_like(bias_own)

    def ring(me, count, k):
        return lax.rem(me + k, count)

    def x_target(p):
        return {"member": y * nx + p}

    def y_target(p):
        return {"member": p * nx + x}

    def z_target(p):
        return {"group": p * CORES + core}

    def add_up(buf, n, first=None):
        acc = buf[0].astype(F32) if first is None else first + buf[0].astype(F32)
        for i in range(1, n):
            acc += buf[i].astype(F32)
        return acc

    def core_copy(h):
        return remote(core_send.at[h], core_recv.at[h], sums, h, sibling)

    def bias_copy():
        return remote(bias_own, bias_core, sums, bias_sem, sibling)

    def layer(h):
        cols = slice(h * awide, (h + 1) * awide)
        late = slice((FCH - 1) * fwide, width)
        total = jnp.zeros((1, awide), F32)
        for b in range(nodes // blk):
            rows = slice(b * blk, (b + 1) * blk)
            p = pre[rows, cols] + dot(neigh[rows, late], w_neigh[late, cols])
            gate = jax.nn.sigmoid(p)
            out[rows, cols] = (p * gate).astype(BF)
            full = cot[rows, cols].astype(F32) * gate * (1.0 + p * (1.0 - gate))
            total = total + jnp.sum(full, axis=0, keepdims=True)
            low[rows, cols] = full.astype(BF)
        for i in range(awide // 128):
            at = h * (awide // 128) + i
            bias_own[at:at + 1, :] = total[:, i * 128:(i + 1) * 128]

    def core_stage(h):
        cols = slice(h * awide, (h + 1) * awide)
        layer(h)
        core_send[h] = dot(left[1 - core], low[:, cols]).astype(BF)
        core_copy(h).start()
        part[h] = dot(left[core], low[:, cols])
        if h == ACH - 1:
            bias_copy().start()

    def x_stage(h):
        core_copy(h).wait()
        total = part[h] + core_recv[h].astype(F32)
        part[h] = total
        x_send[h] = total.astype(BF)
        for k in range(1, nx):
            p = ring(x, nx, k)
            at = pl.ds(pl.multiple_of(p * chunk, chunk), chunk)
            remote(x_send.at[h, at], x_recv.at[h, k - 1], sums, ACH + h, x_target(p)).start()
        if h == ACH - 1:
            bias_copy().wait()
            bias_x[x] = bias_own[...] + bias_core[...]
            for k in range(1, nx):
                p = ring(x, nx, k)
                remote(bias_x.at[x], bias_x.at[x], sums, bias_sem + 1, x_target(p)).start()

    def y_stage(h):
        done(x_recv.at[h], rsem.at[ACH + h])
        total = add_up(x_recv.at[h], nx - 1, part[h, x_rows, :])
        y_full[h] = total
        y_send[h] = total.astype(BF)
        for k in range(1, ny):
            p = ring(y, ny, k)
            at = pl.ds(pl.multiple_of(p * piece, piece), piece)
            remote(y_send.at[h, at], y_recv.at[h, k - 1], sums, 2 * ACH + h, y_target(p)).start()
        if h == ACH - 1:
            done(bias_x.at[pl.ds(0, nx - 1)], rsem.at[bias_sem + 1])
            bias_y[y] = add_up(bias_x, nx)
            for k in range(1, ny):
                p = ring(y, ny, k)
                remote(bias_y.at[y], bias_y.at[y], sums, bias_sem + 2, y_target(p)).start()

    def z_stage(h):
        done(y_recv.at[h], rsem.at[2 * ACH + h])
        z_recv[h, spot] = add_up(y_recv.at[h], ny - 1, y_full[h, y_rows, :]).astype(BF)
        for k in range(1, near):
            p = run * near + ring(spot, near, k)
            remote(z_recv.at[h, spot], z_recv.at[h, spot], sums, 3 * ACH + h, z_target(p)).start()
        if h == ACH - 1:
            done(bias_y.at[pl.ds(0, ny - 1)], rsem.at[bias_sem + 2])
            bias_z[spot] = add_up(bias_y, ny)
            for k in range(1, near):
                p = run * near + ring(spot, near, k)
                remote(bias_z.at[spot], bias_z.at[spot], sums, bias_sem + 3, z_target(p)).start()

    def z_next(h):
        done(z_recv.at[h, pl.ds(0, near - 1)], rsem.at[3 * ACH + h])
        z_last[h, run] = add_up(z_recv.at[h], near).astype(BF)
        for k in range(1, runs):
            p = ring(run, runs, k) * near + spot
            remote(z_last.at[h, run], z_last.at[h, run], sums, 4 * ACH + h, z_target(p)).start()
        if h == ACH - 1:
            done(bias_z.at[pl.ds(0, near - 1)], rsem.at[bias_sem + 3])
            bias_zl[run] = add_up(bias_z, near)
            for k in range(1, runs):
                p = ring(run, runs, k) * near + spot
                remote(bias_zl.at[run], bias_zl.at[run], sums, bias_sem + 4, z_target(p)).start()

    def y_back(h):
        done(z_last.at[h, pl.ds(0, runs - 1)], rsem.at[4 * ACH + h])
        whole[core, h, piece_rows, :] = add_up(z_last.at[h], runs).astype(BF)
        at = whole.at[core, h, piece_rows]
        for k in range(1, ny):
            remote(at, at, sums, 5 * ACH + h, y_target(ring(y, ny, k))).start()

    def x_back(h):
        done(whole.at[0, 0, pl.ds(0, (ny - 1) * piece)], rsem.at[5 * ACH + h])
        at = whole.at[core, h, x_rows]
        for k in range(1, nx):
            remote(at, at, sums, 6 * ACH + h, x_target(ring(x, nx, k))).start()

    def core_back(h):
        done(whole.at[0, 0, pl.ds(0, (nx - 1) * chunk)], rsem.at[6 * ACH + h])
        remote(whole.at[core, h], whole.at[core, h], sums, 7 * ACH + h, sibling).start()

    def member_back(h):
        cols = slice(h * bwide, (h + 1) * bwide)
        for b in range(nodes // blk):
            rows = slice(b * blk, (b + 1) * blk)
            gn = dot(low[rows, :], w_neigh[cols, :], 1, 1) * inv[rows, 0:1]
            hi = gn.astype(BF)
            split[0, rows, :] = hi
            split[1, rows, :] = (gn - hi.astype(F32)).astype(BF)
        back_m[h] = (dot(ref_t[...], split[0]) + dot(ref_t[...], split[1])).astype(BF)

    def member_send(h):
        exchange(back_m.at[h], returned.at[h], 2 * FCH + h, "member", members, m)

    def home(h):
        done(others(returned, members), gsem.at[2 * FCH + h])
        back_z[h] = dot(inner_t[...], returned[h]).astype(BF)
        exchange(back_z.at[h], homeward.at[h], 2 * FCH + BCH + h, "group", groups, g)

    def features_back(h):
        cols = slice(h * bwide, (h + 1) * bwide)
        done(others(homeward, groups), gsem.at[2 * FCH + BCH + h])
        grad_agg = dot(cross_t[...], homeward[h]).astype(BF)
        gfeat[:, cols] = (own[:, cols] + dot(member_t[...], grad_agg)).astype(BF)

    stores = [
        pltpu.make_async_copy(out, out_h, osem.at[0]),
        pltpu.make_async_copy(gfeat, gfeat_h, osem.at[1]),
        pltpu.make_async_copy(gbias, gbias_h, osem.at[2]),
        pltpu.make_async_copy(whole.at[core], grads_h.at[core], osem.at[3]),
    ]
    core_stage(0)
    core_stage(1)
    x_stage(0)
    stores[0].start()
    member_back(0)
    x_stage(1)
    member_back(1)
    member_back(2)
    member_back(3)
    own[...] = dot(low[...], w_self[...], 1, 1)
    y_stage(0)
    y_stage(1)
    member_send(0)
    member_send(1)
    member_send(2)
    member_send(3)
    z_stage(0)
    z_stage(1)
    z_next(0)
    z_next(1)
    home(0)
    home(1)
    y_back(0)
    home(2)
    y_back(1)
    home(3)
    x_back(0)
    x_back(1)
    features_back(0)
    features_back(1)
    features_back(2)
    core_back(0)
    features_back(3)
    core_back(1)
    done(bias_zl.at[pl.ds(0, runs - 1)], rsem.at[bias_sem + 4])
    bias_sum = add_up(bias_zl, runs)
    for i in range(width // 128):
        gbias[:, i * 128:(i + 1) * 128] = bias_sum[i:i + 1, :]
    for store in stores[1:]:
        store.start()
    for h in range(ACH):
        done(whole.at[0, 0], rsem.at[7 * ACH + h])
        late = pltpu.make_async_copy(whole.at[1 - core, h], grads_h.at[1 - core, h], osem.at[4 + h])
        late.start()
        stores.append(late)

    for h in range(FCH):
        done(others(send_z, groups), fsem.at[h])
        done(others(send_m, members), fsem.at[FCH + h])
    for h in range(BCH):
        done(others(back_m, members), fsem.at[2 * FCH + h])
        done(others(back_z, groups), fsem.at[2 * FCH + BCH + h])
    for h in range(ACH):
        done(x_recv.at[h], ssem.at[ACH + h])
        done(y_recv.at[h], ssem.at[2 * ACH + h])
        done(z_recv.at[h, pl.ds(0, near - 1)], ssem.at[3 * ACH + h])
        done(z_last.at[h, pl.ds(0, runs - 1)], ssem.at[4 * ACH + h])
        done(whole.at[0, 0, pl.ds(0, (ny - 1) * piece)], ssem.at[5 * ACH + h])
        done(whole.at[0, 0, pl.ds(0, (nx - 1) * chunk)], ssem.at[6 * ACH + h])
        done(whole.at[0, 0], ssem.at[7 * ACH + h])
    done(bias_x.at[pl.ds(0, nx - 1)], ssem.at[bias_sem + 1])
    done(bias_y.at[pl.ds(0, ny - 1)], ssem.at[bias_sem + 2])
    done(bias_z.at[pl.ds(0, near - 1)], ssem.at[bias_sem + 3])
    done(bias_zl.at[pl.ds(0, runs - 1)], ssem.at[bias_sem + 4])
    for store in stores:
        store.wait()


def finish(out_v, gfeat_v, grads_v, gbias_v, out, gfeat, gws, gwn, gbias, rows, low, full, line, sem):
    wide = grads_v.shape[3]
    parts = [(i, h) for i in range(2) for h in range(ACH)]
    loads = [
        *((grads_v.at[i, h], low.at[i, h]) for i, h in parts),
        (out_v, rows.at[0]), (gfeat_v, rows.at[1]), (gbias_v, line),
    ]
    stores = [
        *((full.at[i, h], (gws, gwn)[i].at[:, pl.ds(h * wide, wide)]) for i, h in parts),
        (rows.at[0], out), (rows.at[1], gfeat), (line, gbias),
    ]
    loads = [pltpu.make_async_copy(a, b, sem.at[i]) for i, (a, b) in enumerate(loads)]
    stores = [pltpu.make_async_copy(a, b, sem.at[len(loads) + i]) for i, (a, b) in enumerate(stores)]
    for load in loads:
        load.start()
    for k, (load, store) in enumerate(zip(loads, stores)):
        load.wait()
        if k < len(parts):
            i, h = parts[k]
            full[i, h] = low[i, h].astype(F32)
        store.start()
    for store in stores:
        store.wait()


def shards(
    nx, features, w_self, w_neigh, bias, set_members, set_size, cross_list, inner_list,
    ref_slot, ref_count, cotangent,
):
    nodes, width = features.shape
    sets, most = set_members.shape
    groups = lax.axis_size("group")
    members = lax.axis_size("member")
    refs = ref_slot.shape[1]
    cap = cross_list.shape[3]
    ny, nz = members // nx, groups // CORES
    near = z_near(nz)
    chunk = width // nx
    piece = chunk // ny
    fwide, bwide, awide = width // FCH, width // BCH, width // ACH
    relays, slots = groups * cap, members * cap
    V = pltpu.VMEM
    S = jax.ShapeDtypeStruct
    outs = pl.pallas_call(
        functools.partial(kernel, groups, members, nx, cap),
        out_shape=(
            S((nodes, width), BF), S((nodes, width), BF), S((2, ACH, width, awide), BF), S((1, width), F32),
        ),
        in_specs=[pl.BlockSpec(memory_space=pl.ANY)] * 11,
        out_specs=(pl.BlockSpec(memory_space=pl.ANY),) * 4,
        scratch_shapes=[
            V((nodes, width), BF), V((width, width), BF), V((width, width), BF), V((1, width), F32),
            V((most, sets), I32), V((1, sets), I32), V((cap, groups), I32), V((cap, members), I32),
            V((refs, nodes), I32), V((1, nodes), I32), V((nodes, width), BF),
            V((nodes, sets), BF), V((sets, nodes), BF),
            V((slots, nodes), BF), V((nodes, slots), BF),
            V((sets, relays), BF), V((relays, sets), BF),
            V((relays, slots), BF), V((slots, relays), BF),
            V((2, width, nodes), BF), V((nodes, 128), F32),
            V((FCH, relays, fwide), BF), V((FCH, relays, fwide), BF),
            V((FCH, slots, fwide), BF), V((FCH, slots, fwide), BF),
            V((nodes, width), BF), V((nodes, width), BF),
            V((nodes, width), F32), V((nodes, width), F32),
            V((2, nodes, bwide), BF),
            V((BCH, slots, bwide), BF), V((BCH, slots, bwide), BF),
            V((BCH, relays, bwide), BF), V((BCH, relays, bwide), BF),
            V((ACH, width, awide), F32),
            V((ACH, width, awide), BF), V((ACH, width, awide), BF), V((ACH, width, awide), BF),
            V((ACH, nx - 1, chunk, awide), BF), V((ACH, chunk, awide), F32), V((ACH, chunk, awide), BF),
            V((ACH, ny - 1, piece, awide), BF), V((ACH, near, piece, awide), BF), V((ACH, nz // near, piece, awide), BF),
            V((2, ACH, width, awide), BF),
            V((nodes, width), BF), V((nodes, width), BF), V((1, width), F32),
            V((8, 128), F32), V((8, 128), F32), V((nx, 8, 128), F32), V((ny, 8, 128), F32),
            V((near, 8, 128), F32), V((nz // near, 8, 128), F32),
            pltpu.SemaphoreType.DMA((11,)),
            pltpu.SemaphoreType.DMA((4 + ACH,)),
            pltpu.SemaphoreType.DMA((8 * ACH + 5,)),
            pltpu.SemaphoreType.DMA((8 * ACH + 5,)),
            pltpu.SemaphoreType.DMA((2 * FCH + 2 * BCH,)),
            pltpu.SemaphoreType.DMA((2 * FCH + 2 * BCH,)),
        ],
        compiler_params=pltpu.CompilerParams(
            collective_id=0, has_side_effects=True, vmem_limit_bytes=60 * 2**20
        ),
    )(
        features, w_self, w_neigh, bias.reshape(1, width), set_members.T, set_size.reshape(1, sets),
        cross_list[0, 0].T, inner_list[0, 0].T, ref_slot.T, ref_count.reshape(1, nodes), cotangent,
    )
    anywhere = pl.BlockSpec(memory_space=pl.ANY)
    output, gfeat, gws, gwn, gbias = pl.pallas_call(
        finish,
        out_shape=(
            S((nodes, width), BF), S((nodes, width), BF), S((width, width), F32), S((width, width), F32),
            S((1, width), F32),
        ),
        in_specs=[anywhere] * 4,
        out_specs=(anywhere,) * 5,
        scratch_shapes=[
            V((2, nodes, width), BF), V((2, ACH, width, awide), BF), V((2, ACH, width, awide), F32), V((1, width), F32),
            pltpu.SemaphoreType.DMA((6 + 4 * ACH,)),
        ],
        compiler_params=pltpu.CompilerParams(vmem_limit_bytes=60 * 2**20),
    )(*outs)
    return output, gfeat, gws, gwn, gbias.reshape(width)


def solution(mesh):
    nx = 4
    in_specs = (
        P(("group", "member"), None),
        P(),
        P(),
        P(),
        P(("group", "member"), None),
        P(("group", "member")),
        P("group", "member", None, None),
        P("group", "member", None, None),
        P(("group", "member"), None),
        P(("group", "member")),
        P(("group", "member"), None),
    )
    out_specs = (P(("group", "member"), None), P(("group", "member"), None), P(), P(), P())
    return jax.shard_map(
        functools.partial(shards, nx), mesh=mesh, in_specs=in_specs, out_specs=out_specs, check_vma=False
    )
```
